32 devices in a mesh: dp: 4 (over y, x), space: 8 (over z, core).
Axes of the slice: x: 2, y: 2, z: 4, core: 2. Of those that a mesh axis runs over, the one named last changes fastest.
Arguments:
- volume: bfloat16 [4, 32, 16, 16, 128], P('dp', None, 'space'), may hold values from -6 to 6
- kernel: bfloat16 [64, 32, 3, 3, 3], replicated, may hold values from -0.21875 to 0.21875
- cotangent: bfloat16 [4, 64, 8, 8, 64], P('dp', None, 'space'), may hold values from -6 to 6
Outputs:
- activated: bfloat16 [4, 64, 8, 8, 64], P('dp', None, 'space')
- grad_volume: bfloat16 [4, 32, 16, 16, 128], P('dp', None, 'space')
- grad_kernel: float32 [64, 32, 3, 3, 3], replicated
The draws below stay inside these ranges and needn't reach their ends.
All inputs are finite; a program needn't handle non-finite values.
Results may differ from the reference program's by a relative error of at most 0.0049.
Values may be sent and summed in bfloat16 or wider, within the bound.
A program may use at most 64 MiB of HBM per device.

```python
import jax
import jax.numpy as jnp
from jax import lax

CIN = 32
COUT = 64
GY = 16
GZ = 128
SAMPLES = 4
GX = 16


def levels(own_key, extent, split, low, high):
    factor_of, own = 1.0, jax.random.fold_in(own_key, 6)
    for dim, shards_of in split:
        steps = jnp.exp(jax.random.uniform(jax.random.fold_in(own, dim), (shards_of,), jnp.float32, low / len(split), high / len(split)))
        factor_of = factor_of * jnp.repeat(steps, extent[dim] // shards_of).reshape([-1 if axis == dim else 1 for axis in range(len(extent))])
    return factor_of


def noise(key, dims, width, limit, cuts=(), dtype=jnp.bfloat16):
    entries = width * jax.random.normal(key, dims, jnp.float32)
    if cuts:
        entries = entries * levels(key, dims, cuts, -0.22, 0.18)
    return jnp.clip(entries, -limit, limit).astype(dtype)


def setup_inputs(seed: int = 0) -> dict:
    splits = jax.random.split(jax.random.key(seed), 4)
    return {
        "volume": noise(splits[0], (SAMPLES, CIN, GX, GY, GZ), 1.0, 6.0, ((0, 4), (2, 8))),
        "kernel": noise(splits[1], (COUT, CIN, 3, 3, 3), (27 * CIN) ** -0.5, 0.21875),
        "cotangent": noise(splits[2], (SAMPLES, COUT, GX // 2, GY // 2, GZ // 2), 1.0, 6.0, ((0, 4), (2, 8))),
    }


def convolve(inputs, weights, precision):
    return lax.conv_general_dilated(inputs, weights, (2, 2, 2), [(1, 1), (1, 1), (1, 1)], dimension_numbers=('NCDHW', 'OIDHW', 'NCDHW'), preferred_element_type=jnp.float32, precision=precision)

def reference(volume, kernel, cotangent):
    pre = convolve(volume, kernel, None)
    activated = (0.01 * pre + 0.99 * jax.nn.softplus(pre)).astype(jnp.bfloat16)
    local_grad = (cotangent.astype(jnp.float32) * (0.01 + 0.99 * jax.nn.sigmoid(pre))).astype(jnp.bfloat16)

    def full_conv(inputs, weights):
        return convolve(inputs, weights, lax.Precision.HIGHEST)
    unused, pullback = jax.vjp(full_conv, volume.astype(jnp.float32), kernel.astype(jnp.float32))
    grad_input, kernel_total = pullback(local_grad.astype(jnp.float32))
    count = SAMPLES * GX * GY * GZ / 8.0
    grad_kernel = kernel_total / jnp.sqrt(jnp.float32(count))
    return (activated, grad_input.astype(jnp.bfloat16), grad_kernel)
```

```python
import functools
import math

import jax
import jax.numpy as jnp
from jax import lax
from jax.experimental import pallas as pl
from jax.experimental.pallas import tpu as pltpu
from jax.sharding import PartitionSpec as P

F32, BF16 = jnp.float32, jnp.bfloat16
MESH = pl.DeviceIdType.MESH


def dot(a, b, contract):
    return lax.dot_general(a, b, ((contract[0], contract[1]), ((), ())), preferred_element_type=F32)


def picks(rows, cols):
    half, z = rows // 128, rows % 128
    c, half_out, cell = cols // 128, (cols // 64) % 2, cols % 64
    return jnp.where((half == half_out) & (z == 2 * cell + c - 1), 1.0, 0.0).astype(BF16)


def spreads(rows, cols):
    half, cell = rows // 64, rows % 64
    c, half_out, z = cols // 256, (cols // 128) % 2, cols % 128
    return jnp.where((half == half_out) & (z == 2 * cell + c - 1), 1.0, 0.0).astype(BF16)


def kernel(nd, ns, root, v_ref, k_ref, c_ref, act_ref, gv_ref, gk_ref,
           halo, vf, vh, left, x_s, cf, gsend, gnext, gz, gout, term,
           recv_a, part, recv_b, gath, full,
           halo_sem, g_sem, send_a, sem_a, send_b, sem_b, send_c, sem_c, send_d, sem_d):
    d, s = lax.axis_index("dp"), lax.axis_index("space")
    ci, co = v_ref.shape[0], c_ref.shape[0]
    sub = term.shape[0] // (nd * ns)
    chunk = sub * ns

    barrier = pltpu.get_barrier_semaphore()
    for k in range(1, nd):
        pl.semaphore_signal(barrier, inc=1, device_id=(lax.rem(d + k, nd), s), device_id_type=MESH)
    for k in range(1, ns):
        pl.semaphore_signal(barrier, inc=1, device_id=(d, lax.rem(s + k, ns)), device_id_type=MESH)

    vf[...] = v_ref[...].astype(F32).reshape(vf.shape)
    pick = picks(lax.broadcasted_iota(jnp.int32, (256, 384), 0), lax.broadcasted_iota(jnp.int32, (256, 384), 1))
    spread = spreads(lax.broadcasted_iota(jnp.int32, (128, 768), 0), lax.broadcasted_iota(jnp.int32, (128, 768), 1))

    pl.semaphore_wait(barrier, nd + ns - 2)

    def up(src, dst):
        return pltpu.make_async_remote_copy(src_ref=src, dst_ref=dst, send_sem=halo_sem.at[0], recv_sem=halo_sem.at[1],
                                            device_id=(d, lax.rem(s + 1, ns)), device_id_type=MESH)

    def down(src, dst):
        return pltpu.make_async_remote_copy(src_ref=src, dst_ref=dst, send_sem=g_sem.at[0], recv_sem=g_sem.at[1],
                                            device_id=(d, lax.rem(s + ns - 1, ns)), device_id_type=MESH)

    @pl.when(s < ns - 1)
    def _():
        up(v_ref.at[:, 1], halo).start()

    def gather_plane(a, ref, first, stride):
        planes = [ref[pl.ds(first + y, ci, stride=stride), :].astype(BF16) for y in range(16)]
        for b in range(3):
            for cell in range(8):
                y, row = 2 * cell + b - 1, ((a * 3 + b) * 4 + cell // 2) * ci
                block = planes[y] if y >= 0 else jnp.zeros((ci, 128), BF16)
                left[row:row + ci, (cell % 2) * 128:(cell % 2) * 128 + 128] = block
        rows = 12 * ci
        picked = dot(left[a * rows:(a + 1) * rows, :], pick, ((1,), (0,))).astype(BF16)
        for b in range(3):
            for j in range(4):
                for c in range(3):
                    row = ((a * 3 + b) * 3 + c) * ci
                    x_s[row:row + ci, j * 128:j * 128 + 128] = picked[(b * 4 + j) * ci:(b * 4 + j + 1) * ci, c * 128:c * 128 + 128]

    gather_plane(1, vf, 0, 32)
    gather_plane(2, vf, 16, 32)
    third = 9 * ci
    pre = dot(k_ref[third:, :], x_s[third:, :], ((0,), (0,)))
    cf[:, :64] = c_ref[...].astype(F32).reshape(co * 8, 64)
    cot = jnp.concatenate(
        [cf[pl.ds(y, co, stride=8), :][:, :64] for y in range(8)], axis=1)

    @pl.when(s > 0)
    def _():
        up(v_ref.at[:, 1], halo).wait_recv()
        vh[...] = halo[...].astype(F32).reshape(vh.shape)

    @pl.when(s == 0)
    def _():
        vh[...] = jnp.zeros_like(vh)

    gather_plane(0, vh, 0, 16)
    pre = pre + dot(k_ref[:third, :], x_s[:third, :], ((0,), (0,)))
    e = jnp.exp(-jnp.abs(pre))
    inverse = 1.0 / (1.0 + e)
    sigmoid = jnp.where(pre >= 0, inverse, e * inverse)
    grad = (cot * (0.01 + 0.99 * sigmoid)).astype(BF16)
    gsend[...] = grad

    @pl.when(s > 0)
    def _():
        down(gsend, gnext).start()

    rows = 27 * ci // 2
    none = jnp.zeros_like(grad)
    term[:rows, :] = dot(x_s[:rows, :], jnp.concatenate([grad, none], axis=0), ((1,), (1,))) + dot(
        x_s[rows:, :], jnp.concatenate([none, grad], axis=0), ((1,), (1,)))
    term[rows:, :] = jnp.zeros((term.shape[0] - rows, 128), F32)

    def copy_a(k):
        to = lax.rem(d + k, nd)
        return pltpu.make_async_remote_copy(
            src_ref=term.at[pl.ds(pl.multiple_of(to * chunk, chunk), chunk)], dst_ref=recv_a.at[k - 1],
            send_sem=send_a.at[k - 1], recv_sem=sem_a.at[k - 1], device_id=(to, s), device_id_type=MESH)

    def copy_b(k):
        to = lax.rem(s + k, ns)
        return pltpu.make_async_remote_copy(
            src_ref=part.at[pl.ds(pl.multiple_of(to * sub, sub), sub)], dst_ref=recv_b.at[k - 1],
            send_sem=send_b.at[k - 1], recv_sem=sem_b.at[k - 1], device_id=(d, to), device_id_type=MESH)

    def copy_c(k):
        return pltpu.make_async_remote_copy(
            src_ref=gath.at[pl.ds(pl.multiple_of(s * sub, sub), sub)],
            dst_ref=gath.at[pl.ds(pl.multiple_of(s * sub, sub), sub)],
            send_sem=send_c.at[k - 1], recv_sem=sem_c.at[k - 1],
            device_id=(d, lax.rem(s + k, ns)), device_id_type=MESH)

    def copy_d(k):
        return pltpu.make_async_remote_copy(
            src_ref=gath, dst_ref=full.at[pl.ds(pl.multiple_of(d * chunk, chunk), chunk)],
            send_sem=send_d.at[k - 1], recv_sem=sem_d.at[k - 1],
            device_id=(lax.rem(d + k, nd), s), device_id_type=MESH)

    for k in range(1, nd):
        copy_a(k).start()

    softplus = jnp.maximum(pre, 0.0) + jnp.log1p(e)
    act = 0.01 * pre + 0.99 * softplus
    for j in range(4):
        pair = act[:, j * 128:j * 128 + 128]
        cf[pl.ds(2 * j, co, stride=8), :] = pair
        cf[pl.ds(2 * j + 1, co, stride=8), :] = pltpu.roll(pair, 64, 1)
    act_ref[...] = cf[:, :64].reshape(act_ref.shape).astype(BF16)

    def grad_rows(a_list, g):
        stacked = jnp.concatenate([g[:, j * 128:j * 128 + 128] for j in range(4)], axis=0)
        wide = dot(stacked, spread, ((1,), (0,))).astype(BF16)
        for c in range(3):
            for j in range(4):
                gz[c * co:(c + 1) * co, j * 256:j * 256 + 256] = wide[j * co:(j + 1) * co, c * 256:c * 256 + 256]
        total = None
        for c in range(3):
            weights = jnp.concatenate(
                [k_ref[((a * 3 + b) * 3 + c) * ci:((a * 3 + b) * 3 + c + 1) * ci, :] for a in a_list for b in range(3)], axis=0)
            one = dot(weights, gz[c * co:(c + 1) * co, :], ((1,), (0,)))
            total = one if total is None else total + one
        return total

    def tile(total, which, y):
        m = y // 2

        def at(b, cell):
            row = (which * 3 + b) * ci
            return total[row:row + ci, cell * 128:cell * 128 + 128]

        if y % 2 == 0:
            return at(1, m)
        return at(2, m) + at(0, m + 1) if m < 7 else at(2, m)

    own = grad_rows((1, 2), grad)
    for p in range(2):
        for y in range(16):
            gout[pl.ds(p * 16 + y, ci, stride=32), :] = tile(own, p, y)

    for k in range(1, nd):
        copy_a(k).wait_recv()
    total = term[pl.ds(pl.multiple_of(d * chunk, chunk), chunk), :]
    for k in range(1, nd):
        total = total + recv_a[k - 1]
    part[...] = total
    for k in range(1, ns):
        copy_b(k).start()

    @pl.when(s < ns - 1)
    def _():
        down(gsend, gnext).wait_recv()
        above = grad_rows((0,), gnext[...])
        for y in range(16):
            where = pl.ds(16 + y, ci, stride=32)
            gout[where, :] = gout[where, :] + tile(above, 0, y)

    gv_ref[...] = gout[...].astype(BF16).reshape(gv_ref.shape)

    for k in range(1, ns):
        copy_b(k).wait_recv()
    total = part[pl.ds(pl.multiple_of(s * sub, sub), sub), :]
    for k in range(1, ns):
        total = total + recv_b[k - 1]
    gath[pl.ds(pl.multiple_of(s * sub, sub), sub), :] = (total / root).astype(gath.dtype)
    for k in range(1, ns):
        copy_c(k).start()
    for k in range(1, ns):
        copy_c(k).wait_recv()
    for k in range(1, nd):
        copy_d(k).start()
    full[pl.ds(pl.multiple_of(d * chunk, chunk), chunk), :] = gath[...]
    for k in range(1, nd):
        copy_d(k).wait_recv()
    packed = full[:rows, :].astype(F32)
    gk_ref[:rows, :] = packed[:, :64]
    gk_ref[rows:, :] = packed[:, 64:]

    @pl.when(s < ns - 1)
    def _():
        up(v_ref.at[:, 1], halo).wait_send()

    @pl.when(s > 0)
    def _():
        down(gsend, gnext).wait_send()

    for k in range(1, nd):
        copy_a(k).wait_send()
        copy_d(k).wait_send()
    for k in range(1, ns):
        copy_b(k).wait_send()
        copy_c(k).wait_send()


def per_device(volume, weights, cotangent):
    nd, ns = lax.axis_size("dp"), lax.axis_size("space")
    _, ci, planes, gy, gz_ = volume.shape
    co = weights.shape[0]
    cells = volume.shape[0] * nd * planes * ns * gy * gz_ / 8.0
    sub = 16 * max(1, -(-(27 * ci // 2) // (16 * nd * ns)))
    chunk, rows = sub * ns, sub * ns * nd
    dma = pltpu.SemaphoreType.DMA
    vmem = pl.BlockSpec(memory_space=pltpu.VMEM)
    k2 = weights.transpose(2, 3, 4, 1, 0).reshape(27 * ci, co)
    act, gv, gk = pl.pallas_call(
        functools.partial(kernel, nd, ns, math.sqrt(cells)),
        out_shape=(
            jax.ShapeDtypeStruct((co, gy // 2, gz_ // 2), BF16),
            jax.ShapeDtypeStruct((ci, planes, gy, gz_), BF16),
            jax.ShapeDtypeStruct((27 * ci, co), F32),
        ),
        in_specs=[vmem] * 3,
        out_specs=(vmem,) * 3,
        scratch_shapes=[
            pltpu.VMEM((ci, gy, gz_), BF16),
            pltpu.VMEM((ci * 2 * gy, gz_), F32),
            pltpu.VMEM((ci * gy, gz_), F32),
            pltpu.VMEM((36 * ci, 256), BF16),
            pltpu.VMEM((27 * ci, 512), BF16),
            pltpu.VMEM((co * 8, 128), F32),
            pltpu.VMEM((co, 512), BF16),
            pltpu.VMEM((co, 512), BF16),
            pltpu.VMEM((3 * co, 1024), BF16),
            pltpu.VMEM((ci * 2 * gy, gz_), F32),
            pltpu.VMEM((rows, 128), F32),
            pltpu.VMEM((nd - 1, chunk, 128), F32),
            pltpu.VMEM((chunk, 128), F32),
            pltpu.VMEM((ns - 1, sub, 128), F32),
            pltpu.VMEM((chunk, 128), BF16),
            pltpu.VMEM((rows, 128), BF16),
            dma((2,)), dma((2,)),
            dma((nd - 1,)), dma((nd - 1,)), dma((ns - 1,)), dma((ns - 1,)),
            dma((ns - 1,)), dma((ns - 1,)), dma((nd - 1,)), dma((nd - 1,)),
        ],
        compiler_params=pltpu.CompilerParams(collective_id=0, has_side_effects=True, vmem_limit_bytes=44 * 2**20),
        cost_estimate=pl.CostEstimate(flops=400_000_000, bytes_accessed=1_500_000, transcendentals=100_000),
    )(volume[0], k2, cotangent[0, :, 0])
    grad_kernel = gk.reshape(3, 3, 3, ci, co).transpose(4, 3, 0, 1, 2)
    return act[None, :, None], gv[None], grad_kernel


def solution(mesh):
    split = P("dp", None, "space", None, None)
    return jax.shard_map(
        per_device, mesh=mesh, in_specs=(split, P(), split), out_specs=(split, split, P()), check_vma=False)
```

```python
import functools
import math

import jax
import jax.numpy as jnp
from jax import lax
from jax.experimental import pallas as pl
from jax.experimental.pallas import tpu as pltpu
from jax.sharding import PartitionSpec as P

F32, BF16 = jnp.float32, jnp.bfloat16
MESH = pl.DeviceIdType.MESH


def dot(a, b, contract):
    return lax.dot_general(a, b, ((contract[0], contract[1]), ((), ())), preferred_element_type=F32)


def picks(rows, cols):
    half, z = rows // 128, rows % 128
    c, half_out, cell = cols // 128, (cols // 64) % 2, cols % 64
    return jnp.where((half == half_out) & (z == 2 * cell + c - 1), 1.0, 0.0).astype(BF16)


def spreads(rows, cols):
    half, cell = rows // 64, rows % 64
    c, half_out, z = cols // 256, (cols // 128) % 2, cols % 128
    return jnp.where((half == half_out) & (z == 2 * cell + c - 1), 1.0, 0.0).astype(BF16)


def kernel(nd, ns, root, v_hbm, k_hbm, c_hbm, act_hbm, gv_hbm, gk_hbm,
           v_ref, k_ref, c_ref, in_sem, act_ref, gv_ref, out_sem, halo, vf, vh, left, x_s, cf, gsend, gnext, gz, gout, term,
           recv_a, part, recv_b, full,
           halo_sem, g_sem, send_a, sem_a, send_b, sem_b, send_c, sem_c):
    d, s = lax.axis_index("dp"), lax.axis_index("space")
    ci, co = v_ref.shape[0], c_ref.shape[0]
    pair, line = 2, ns // 2
    group, chunk = nd * pair, term.shape[0] // (nd * pair)
    core, z = lax.rem(s, pair), s // pair
    other = lax.rem(s + (ns - 1) - core * (ns - 2), ns)

    def near(k):
        return lax.rem(d + k // pair, nd), z * pair + lax.rem(core + k % pair, pair)

    def along(k):
        return d, lax.rem(z + k, line) * pair + core

    def slot(to):
        return pl.ds(pl.multiple_of((to[0] * pair + lax.rem(to[1], pair)) * chunk, chunk), chunk)

    mine = slot((d, s))

    fetch_v = pltpu.make_async_copy(v_hbm, v_ref, in_sem.at[0])
    fetch_k = pltpu.make_async_copy(k_hbm, k_ref, in_sem.at[1])
    fetch_c = pltpu.make_async_copy(c_hbm, c_ref, in_sem.at[2])
    fetch_v.start()
    fetch_k.start()
    fetch_c.start()
    barrier = pltpu.get_barrier_semaphore()
    for to in [near(k) for k in range(1, group)] + [along(k) for k in range(1, line)]:
        pl.semaphore_signal(barrier, inc=1, device_id=to, device_id_type=MESH)
    pl.semaphore_signal(barrier, inc=1, device_id=(d, other), device_id_type=MESH)

    pick = picks(lax.broadcasted_iota(jnp.int32, (256, 384), 0), lax.broadcasted_iota(jnp.int32, (256, 384), 1))
    spread = spreads(lax.broadcasted_iota(jnp.int32, (128, 768), 0), lax.broadcasted_iota(jnp.int32, (128, 768), 1))

    pl.semaphore_wait(barrier, group + line - 1)

    def up(src, dst):
        return pltpu.make_async_remote_copy(src_ref=src, dst_ref=dst, send_sem=halo_sem.at[0], recv_sem=halo_sem.at[1],
                                            device_id=(d, lax.rem(s + 1, ns)), device_id_type=MESH)

    def down(src, dst):
        return pltpu.make_async_remote_copy(src_ref=src, dst_ref=dst, send_sem=g_sem.at[0], recv_sem=g_sem.at[1],
                                            device_id=(d, lax.rem(s + ns - 1, ns)), device_id_type=MESH)

    @pl.when(s < ns - 1)
    def _():
        up(v_hbm.at[:, 1], halo).start()

    fetch_v.wait()
    vf[...] = v_ref[...].astype(F32).reshape(vf.shape)

    def gather_plane(a, ref, first, stride):
        planes = [ref[pl.ds(first + y, ci, stride=stride), :].astype(BF16) for y in range(16)]
        for b in range(3):
            for cell in range(8):
                y, row = 2 * cell + b - 1, ((a * 3 + b) * 4 + cell // 2) * ci
                block = planes[y] if y >= 0 else jnp.zeros((ci, 128), BF16)
                left[row:row + ci, (cell % 2) * 128:(cell % 2) * 128 + 128] = block
        rows = 12 * ci
        picked = dot(left[a * rows:(a + 1) * rows, :], pick, ((1,), (0,))).astype(BF16)
        for b in range(3):
            for j in range(4):
                for c in range(3):
                    row = ((a * 3 + b) * 3 + c) * ci
                    x_s[row:row + ci, j * 128:j * 128 + 128] = picked[(b * 4 + j) * ci:(b * 4 + j + 1) * ci, c * 128:c * 128 + 128]

    gather_plane(1, vf, 0, 32)
    gather_plane(2, vf, 16, 32)
    third = 9 * ci
    fetch_k.wait()
    fetch_c.wait()
    pre = dot(k_ref[third:, :], x_s[third:, :], ((0,), (0,)))
    cf[:, :64] = c_ref[...].astype(F32).reshape(co * 8, 64)
    cot = jnp.concatenate(
        [cf[pl.ds(y, co, stride=8), :][:, :64] for y in range(8)], axis=1)

    @pl.when(s > 0)
    def _():
        up(v_hbm.at[:, 1], halo).wait_recv()
        vh[...] = halo[...].astype(F32).reshape(vh.shape)

    @pl.when(s == 0)
    def _():
        vh[...] = jnp.zeros_like(vh)

    gather_plane(0, vh, 0, 16)
    pre = pre + dot(k_ref[:third, :], x_s[:third, :], ((0,), (0,)))
    e = jnp.exp(-jnp.abs(pre))
    inverse = 1.0 / (1.0 + e)
    sigmoid = jnp.where(pre >= 0, inverse, e * inverse)
    grad = (cot * (0.01 + 0.99 * sigmoid)).astype(BF16)
    gsend[...] = grad

    @pl.when(s > 0)
    def _():
        down(gsend, gnext).start()

    rows = 27 * ci // 2
    none = jnp.zeros_like(grad)
    term[:rows, :] = dot(x_s[:rows, :], jnp.concatenate([grad, none], axis=0), ((1,), (1,))) + dot(
        x_s[rows:, :], jnp.concatenate([none, grad], axis=0), ((1,), (1,)))
    term[rows:, :] = jnp.zeros((term.shape[0] - rows, 128), F32)

    def copy_a(k):
        to = near(k)
        return pltpu.make_async_remote_copy(
            src_ref=term.at[slot(to)], dst_ref=recv_a.at[k - 1],
            send_sem=send_a.at[k - 1], recv_sem=sem_a.at[k - 1], device_id=to, device_id_type=MESH)

    def copy_b(k):
        return pltpu.make_async_remote_copy(
            src_ref=part, dst_ref=recv_b.at[k - 1],
            send_sem=send_b.at[k - 1], recv_sem=sem_b.at[k - 1], device_id=along(k), device_id_type=MESH)

    def copy_c(k):
        return pltpu.make_async_remote_copy(
            src_ref=full.at[mine], dst_ref=full.at[mine],
            send_sem=send_c.at[k - 1], recv_sem=sem_c.at[k - 1], device_id=near(k), device_id_type=MESH)

    for k in range(1, group):
        copy_a(k).start()

    softplus = jnp.maximum(pre, 0.0) + jnp.log1p(e)
    act = 0.01 * pre + 0.99 * softplus
    for j in range(4):
        both = act[:, j * 128:j * 128 + 128]
        cf[pl.ds(2 * j, co, stride=8), :] = both
        cf[pl.ds(2 * j + 1, co, stride=8), :] = pltpu.roll(both, 64, 1)
    act_ref[...] = cf[:, :64].reshape(act_ref.shape).astype(BF16)
    store_act = pltpu.make_async_copy(act_ref, act_hbm, out_sem.at[0])
    store_act.start()

    def grad_rows(a_list, g):
        stacked = jnp.concatenate([g[:, j * 128:j * 128 + 128] for j in range(4)], axis=0)
        wide = dot(stacked, spread, ((1,), (0,))).astype(BF16)
        for c in range(3):
            for j in range(4):
                gz[c * co:(c + 1) * co, j * 256:j * 256 + 256] = wide[j * co:(j + 1) * co, c * 256:c * 256 + 256]
        total = None
        for c in range(3):
            weights = jnp.concatenate(
                [k_ref[((a * 3 + b) * 3 + c) * ci:((a * 3 + b) * 3 + c + 1) * ci, :] for a in a_list for b in range(3)], axis=0)
            one = dot(weights, gz[c * co:(c + 1) * co, :], ((1,), (0,)))
            total = one if total is None else total + one
        return total

    def tile(total, which, y):
        m = y // 2

        def at(b, cell):
            row = (which * 3 + b) * ci
            return total[row:row + ci, cell * 128:cell * 128 + 128]

        if y % 2 == 0:
            return at(1, m)
        return at(2, m) + at(0, m + 1) if m < 7 else at(2, m)

    own = grad_rows((1, 2), grad)
    for p in range(2):
        for y in range(16):
            gout[pl.ds(p * 16 + y, ci, stride=32), :] = tile(own, p, y)

    for k in range(1, group):
        copy_a(k).wait_recv()
    total = term[mine, :]
    for k in range(1, group):
        total = total + recv_a[k - 1]
    part[...] = total
    for k in range(1, line):
        copy_b(k).start()

    @pl.when(s < ns - 1)
    def _():
        down(gsend, gnext).wait_recv()
        above = grad_rows((0,), gnext[...])
        for y in range(16):
            where = pl.ds(16 + y, ci, stride=32)
            gout[where, :] = gout[where, :] + tile(above, 0, y)

    gv_ref[...] = gout[...].astype(BF16).reshape(gv_ref.shape)
    store_gv = pltpu.make_async_copy(gv_ref, gv_hbm, out_sem.at[1])
    store_gv.start()

    for k in range(1, line):
        copy_b(k).wait_recv()
    total = part[...]
    for k in range(1, line):
        total = total + recv_b[k - 1]
    full[mine, :] = (total / root).astype(full.dtype)
    for k in range(1, group):
        copy_c(k).start()
    for k in range(1, group):
        copy_c(k).wait_recv()
    store_gk = pltpu.make_async_copy(full, gk_hbm, out_sem.at[2])
    store_gk.start()
    @pl.when(s < ns - 1)
    def _():
        up(v_hbm.at[:, 1], halo).wait_send()

    @pl.when(s > 0)
    def _():
        down(gsend, gnext).wait_send()

    for k in range(1, group):
        copy_a(k).wait_send()
        copy_c(k).wait_send()
    for k in range(1, line):
        copy_b(k).wait_send()
    store_act.wait()
    store_gv.wait()
    store_gk.wait()


def put(act, gv, packed, act_out, gv_out, gk_out, act_v, gv_v, packed_v, gk_v, sem):
    loads = [pltpu.make_async_copy(x, y, sem.at[i]) for i, (x, y) in enumerate(((packed, packed_v), (gv, gv_v), (act, act_v)))]
    stores = [pltpu.make_async_copy(x, y, sem.at[i + 3]) for i, (x, y) in enumerate(((gk_v, gk_out), (gv_v, gv_out), (act_v, act_out)))]
    for load in loads:
        load.start()
    loads[0].wait()
    rows = gk_v.shape[0] // 2
    gk_v[:rows, :] = packed_v[:rows, :64].astype(F32)
    gk_v[rows:, :] = packed_v[:rows, 64:].astype(F32)
    stores[0].start()
    for load, store in zip(loads[1:], stores[1:]):
        load.wait()
        store.start()
    for store in stores:
        store.wait()


def per_device(volume, weights, cotangent):
    nd, ns = lax.axis_size("dp"), lax.axis_size("space")
    _, ci, planes, gy, gz_ = volume.shape
    co = weights.shape[0]
    cells = volume.shape[0] * nd * planes * ns * gy * gz_ / 8.0
    group, line = nd * 2, ns // 2
    chunk = 16 * max(1, -(-(27 * ci // 2) // (16 * group)))
    rows = chunk * group
    dma = pltpu.SemaphoreType.DMA
    hbm = pl.BlockSpec(memory_space=pltpu.HBM)
    k2 = weights.transpose(2, 3, 4, 1, 0).reshape(27 * ci, co)
    act, gv, packed = pl.pallas_call(
        functools.partial(kernel, nd, ns, math.sqrt(cells)),
        out_shape=(
            jax.ShapeDtypeStruct((co, gy // 2, gz_ // 2), BF16),
            jax.ShapeDtypeStruct((ci, planes, gy, gz_), BF16),
            jax.ShapeDtypeStruct((rows, 128), BF16),
        ),
        in_specs=[hbm] * 3,
        out_specs=(hbm,) * 3,
        scratch_shapes=[
            pltpu.VMEM((ci, planes, gy, gz_), BF16),
            pltpu.VMEM((27 * ci, co), BF16),
            pltpu.VMEM((co, gy // 2, gz_ // 2), BF16),
            dma((3,)),
            pltpu.VMEM((co, gy // 2, gz_ // 2), BF16),
            pltpu.VMEM((ci, planes, gy, gz_), BF16),
            dma((3,)),
            pltpu.VMEM((ci, gy, gz_), BF16),
            pltpu.VMEM((ci * 2 * gy, gz_), F32),
            pltpu.VMEM((ci * gy, gz_), F32),
            pltpu.VMEM((36 * ci, 256), BF16),
            pltpu.VMEM((27 * ci, 512), BF16),
            pltpu.VMEM((co * 8, 128), F32),
            pltpu.VMEM((co, 512), BF16),
            pltpu.VMEM((co, 512), BF16),
            pltpu.VMEM((3 * co, 1024), BF16),
            pltpu.VMEM((ci * 2 * gy, gz_), F32),
            pltpu.VMEM((rows, 128), F32),
            pltpu.VMEM((group - 1, chunk, 128), F32),
            pltpu.VMEM((chunk, 128), F32),
            pltpu.VMEM((line - 1, chunk, 128), F32),
            pltpu.VMEM((rows, 128), BF16),
            dma((2,)), dma((2,)),
            dma((group - 1,)), dma((group - 1,)), dma((line - 1,)), dma((line - 1,)),
            dma((group - 1,)), dma((group - 1,)),
        ],
        compiler_params=pltpu.CompilerParams(collective_id=0, has_side_effects=True, vmem_limit_bytes=60 * 2**20),
        cost_estimate=pl.CostEstimate(flops=400_000_000, bytes_accessed=1_500_000, transcendentals=100_000),
    )(volume[0], k2, cotangent[0, :, 0])
    act, gv, gk = pl.pallas_call(
        put,
        out_shape=(
            jax.ShapeDtypeStruct(act.shape, BF16),
            jax.ShapeDtypeStruct(gv.shape, BF16),
            jax.ShapeDtypeStruct((27 * ci, co), F32),
        ),
        in_specs=[hbm] * 3,
        out_specs=(hbm,) * 3,
        scratch_shapes=[
            pltpu.VMEM(act.shape, BF16),
            pltpu.VMEM(gv.shape, BF16),
            pltpu.VMEM(packed.shape, BF16),
            pltpu.VMEM((27 * ci, co), F32),
            dma((6,)),
        ],
        compiler_params=pltpu.CompilerParams(vmem_limit_bytes=60 * 2**20),
    )(act, gv, packed)
    grad_kernel = gk.reshape(3, 3, 3, ci, co).transpose(4, 3, 0, 1, 2)
    return act[None, :, None], gv[None], grad_kernel


def solution(mesh):
    split = P("dp", None, "space", None, None)
    return jax.shard_map(
        per_device, mesh=mesh, in_specs=(split, P(), split), out_specs=(split, split, P()), check_vma=False)
```
